128 devices in a mesh: shards: 8 (over x, z_lo), context: 16 (over y, z_hi, core).
Axes of the slice: x: 4, y: 4, z: 4 (z_hi: 2, z_lo: 2; z = z_hi * 2 + z_lo), core: 2. Of those that a mesh axis runs over, the one named last changes fastest.
Arguments:
- hidden_in: bfloat16 [8, 2048, 1024], P('shards', 'context'), may hold values from -6 to 6
- ln_gain: float32 [2, 1024], replicated, may hold values from 0.5 to 1.5
- ln_bias: float32 [2, 1024], replicated, may hold values from -1.75 to 1.75
- qkv_weight: bfloat16 [2, 1024, 16, 192], P(None, 'shards', 'context'), may hold values from -0.1875 to 0.1875
- qkv_bias: float32 [2, 16, 192], replicated, may hold values from -1.75 to 1.75
- out_weight: bfloat16 [2, 16, 64, 1024], P(None, 'context', None, 'shards'), may hold values from -1.5 to 1.5
- out_bias: float32 [2, 1024], replicated, may hold values from -1.75 to 1.75
- fc1_weight: bfloat16 [2, 1024, 4096], P(None, 'shards', 'context'), may hold values from -0.1875 to 0.1875
- fc1_bias: float32 [2, 4096], replicated, may hold values from -3 to 3
- fc2_weight: bfloat16 [2, 4096, 1024], P(None, 'context', 'shards'), may hold values from -0.09375 to 0.09375
- fc2_bias: float32 [2, 1024], replicated, may hold values from -1.75 to 1.75
- cotangent: bfloat16 [8, 2048, 1024], P('shards', 'context'), may hold values from -6 to 6
Outputs:
- hidden_out: bfloat16 [8, 2048, 1024], P('shards', 'context')
- grad_in: float32 [8, 2048, 1024], P('shards', 'context')
- grad_ln_gain: float32 [2, 1024], replicated
- grad_ln_bias: float32 [2, 1024], replicated
- grad_qkv_weight: float32 [2, 1024, 16, 192], P(None, 'shards', 'context')
- grad_qkv_bias: float32 [2, 16, 192], replicated
- grad_out_weight: float32 [2, 16, 64, 1024], P(None, 'context', None, 'shards')
- grad_out_bias: float32 [2, 1024], replicated
- grad_fc1_weight: float32 [2, 1024, 4096], P(None, 'shards', 'context')
- grad_fc1_bias: float32 [2, 4096], replicated
- grad_fc2_weight: float32 [2, 4096, 1024], P(None, 'context', 'shards')
- grad_fc2_bias: float32 [2, 1024], replicated
The draws below stay inside these ranges and needn't reach their ends.
All inputs are finite; a program needn't handle non-finite values.
Results may differ from the reference program's by a relative error of at most 0.028.
Values may be sent and summed in bfloat16 or wider, within the bound.
A program may use at most 192 MiB of HBM per device.

```python
import jax
import jax.numpy as jnp
from jax import lax

D = 1024
HEADS = 16
HD = 64
FF = 4096
ROT = 16
LAYERS = 2
SEQS = 8
SEQ = 2048


def block_scale(stream_key, dims, split, low, largest):
    def one(dim, parts):
        heights = jax.random.uniform(jax.random.fold_in(jax.random.fold_in(stream_key, 6), dim), (parts,), jnp.float32, low / len(split), largest / len(split))
        return jnp.repeat(jnp.exp(heights), dims[dim] // parts).reshape((-1,) + (1,) * (len(dims) - dim - 1))

    level = one(*split[0])
    for cut in split[1:]:
        level = level * one(*cut)
    return level


def normal_values(rng, extent, spread, bound, shards=(), held_as=jnp.bfloat16):
    level = block_scale(rng, extent, shards, -0.22, 0.18) if shards else 1.0
    values = jax.random.normal(rng, extent, jnp.float32) * spread * level
    return jnp.minimum(jnp.maximum(values, -bound), bound).astype(held_as)


def setup_inputs(seed: int = 0) -> dict:
    key_of = jax.random.split(jax.random.key(seed), 13)
    hidden_in = normal_values(key_of[0], (SEQS, SEQ, D), 1.0, 6.0, ((0, 8), (1, 16)))
    ln_gain = jnp.clip(1.0 + 0.1 * jax.random.normal(key_of[1], (LAYERS, D), jnp.float32), 0.5, 1.5)
    ln_bias = normal_values(key_of[2], (LAYERS, D), 0.3, 1.75, (), jnp.float32)
    qkv_weight = normal_values(key_of[3], (LAYERS, D, HEADS, 3 * HD), D ** -0.5, 0.1875, ((1, 8), (2, 16)))
    qkv_bias = normal_values(key_of[4], (LAYERS, HEADS, 3 * HD), 0.3, 1.75, (), jnp.float32)
    out_weight = normal_values(key_of[5], (LAYERS, HEADS, HD, D), (max(1, D // 64)) ** -0.5, 1.5, ((1, 16), (3, 8)))
    out_bias = normal_values(key_of[6], (LAYERS, D), 0.3, 1.75, (), jnp.float32)
    fc1_weight = normal_values(key_of[7], (LAYERS, D, FF), D ** -0.5, 0.1875, ((1, 8), (2, 16)))
    fc1_bias = normal_values(key_of[8], (LAYERS, FF), 0.5, 3.0, (), jnp.float32)
    fc2_weight = normal_values(key_of[9], (LAYERS, FF, D), FF ** -0.5, 0.09375, ((1, 16), (2, 8)))
    fc2_bias = normal_values(key_of[10], (LAYERS, D), 0.3, 1.75, (), jnp.float32)
    cotangent = normal_values(key_of[11], (SEQS, SEQ, D), 1.0, 6.0, ((0, 8), (1, 16)))
    return {"hidden_in": hidden_in, "ln_gain": ln_gain, "ln_bias": ln_bias, "qkv_weight": qkv_weight, "qkv_bias": qkv_bias, "out_weight": out_weight, "out_bias": out_bias, "fc1_weight": fc1_weight, "fc1_bias": fc1_bias, "fc2_weight": fc2_weight, "fc2_bias": fc2_bias, "cotangent": cotangent}


@jax.custom_vjp
def low(v):
    return lax.optimization_barrier(v.astype(jnp.bfloat16)).astype(jnp.float32)

@jax.custom_vjp
def low_back(v):
    return v

def low_keep(v):
    return (low(v), None)

def low_pass(kept, grad):
    return (grad,)

def back_keep(v):
    return (v, None)

def back_low(kept, grad):
    return (low(grad),)
low.defvjp(low_keep, low_pass)
low_back.defvjp(back_keep, back_low)

def layer_norm(rows_in, gain_vec, shift_vec):
    row_mean = lax.optimization_barrier(jnp.mean(rows_in, axis=-1, keepdims=True))
    centered = rows_in - row_mean
    variance = lax.optimization_barrier(jnp.mean(centered * centered, axis=-1, keepdims=True))
    return centered * lax.rsqrt(variance + 1e-05) * gain_vec + shift_vec

def rotary_tables(length):
    frequency = 1.0 / 10000.0 ** (jnp.arange(0, ROT, 2).astype(jnp.float32) / ROT)
    angles = jnp.arange(length).astype(jnp.float32)[:, None] * frequency[None, :]
    return (jnp.cos(angles)[:, None, :], jnp.sin(angles)[:, None, :])

def rotate(section, cosine, sine_table):
    half_rot = ROT // 2
    front_half = section[..., :half_rot]
    back_half = section[..., half_rot:ROT]
    remainder = section[..., ROT:]
    return jnp.concatenate([front_half * cosine - back_half * sine_table, back_half * cosine + front_half * sine_table, remainder], axis=-1)

def attention(queries, key_rows, values):
    length = queries.shape[0]
    block_rows = min(512, length)
    scaling = HD ** (-0.5)
    key_pos = jnp.arange(length, dtype=jnp.int32)

    def one_block(block_index):
        begin_row = (block_index * block_rows).astype(jnp.int32)
        query_block = lax.dynamic_slice_in_dim(queries, begin_row, block_rows, 0)
        scores = jnp.einsum('qhd,khd->hqk', query_block, key_rows, precision=lax.Precision.HIGHEST) * scaling
        scores = low_back(scores)
        query_pos = begin_row + jnp.arange(block_rows, dtype=jnp.int32)
        allowed = key_pos[None, :] <= query_pos[:, None]
        scores = jnp.where(allowed[None], scores, -1e+30)
        weights = low(jax.nn.softmax(scores, axis=-1))
        return jnp.einsum('hqk,khd->qhd', weights, values, precision=lax.Precision.HIGHEST)
    blocks = lax.map(jax.checkpoint(one_block), jnp.arange(length // block_rows, dtype=jnp.int32))
    return blocks.reshape(length, queries.shape[1], queries.shape[2])

def apply_layer(stream, layer_params, cosine, sine_table):
    gain_vec, shift_vec, w_qkv, bias_qkv, w_out, bias_out, w_up, bias_up, w_down, bias_down = layer_params
    normed = low(layer_norm(stream, gain_vec, shift_vec))
    projected = jnp.einsum('td,dhe->the', normed, w_qkv, precision=lax.Precision.HIGHEST)
    projected = low_back(projected + bias_qkv)
    queries = low(rotate(projected[..., :HD], cosine, sine_table))
    key_rows = low(rotate(projected[..., HD:2 * HD], cosine, sine_table))
    values = low(projected[..., 2 * HD:])
    mixed = low(low_back(attention(queries, key_rows, values)))
    hidden = low_back(jnp.dot(normed, w_up, precision=lax.Precision.HIGHEST) + bias_up)
    active = low(jax.nn.gelu(hidden, approximate=False))
    branch = jnp.einsum('thd,hde->te', mixed, w_out, precision=lax.Precision.HIGHEST)
    branch = branch + jnp.dot(active, w_down, precision=lax.Precision.HIGHEST) + bias_out + bias_down
    return stream + low_back(branch)

def forward(params, rows_in, cosine, sine_table):
    stream = rows_in
    for layer_index in range(LAYERS):
        stream = apply_layer(stream, [tensor[layer_index] for tensor in params], cosine, sine_table)
    return stream

def reference(hidden_in, ln_gain, ln_bias, qkv_weight, qkv_bias, out_weight, out_bias, fc1_weight, fc1_bias, fc2_weight, fc2_bias, cotangent):
    params = tuple((tensor.astype(jnp.float32) for tensor in (ln_gain, ln_bias, qkv_weight, qkv_bias, out_weight, out_bias, fc1_weight, fc1_bias, fc2_weight, fc2_bias)))
    cosine, sine_table = rotary_tables(hidden_in.shape[1])

    def run_forward(weights_in, rows_in):
        return forward(weights_in, rows_in, cosine, sine_table)

    def one_sequence(totals, seq_pair):
        rows_in, grad_out = seq_pair
        result, pull_back = jax.vjp(run_forward, params, rows_in.astype(jnp.float32))
        grads, grad_rows = pull_back(grad_out.astype(jnp.float32))
        totals = jax.tree.map(lambda first, second: first + second, totals, grads)
        return (totals, (result.astype(jnp.bfloat16), grad_rows))
    zero_totals = jax.tree.map(jnp.zeros_like, params)
    totals, outputs = lax.scan(one_sequence, zero_totals, (hidden_in, cotangent))
    hidden_out, grad_in = outputs
    grad_gain, grad_shift, grad_qkv, grad_qkv_b, grad_out_w, grad_out_b, grad_up_w, grad_up_b, grad_down_w, grad_down_b = totals
    return (hidden_out, grad_in, grad_gain, grad_shift, grad_qkv, grad_qkv_b, grad_out_w, grad_out_b, grad_up_w, grad_up_b, grad_down_w, grad_down_b)
```

```python
import jax
import jax.numpy as jnp
import numpy as np
from jax import lax
from jax.experimental import pallas as pl
from jax.experimental.pallas import tpu as pltpu
from jax.sharding import PartitionSpec as P

HD = 64
ROT = 16
LAYERS = 2
EPSILON = 1e-05
MASKED = -1e30
MESH = pl.DeviceIdType.MESH
F32 = jnp.float32
BF16 = jnp.bfloat16
VMEM_LIMIT = 127 * 512 * 1024
IN_ROWS = slice(0, 448)
OUT_ROWS = slice(448, 768)
ORDER = (2, 1, -1, 0)
ARRIVAL = (0, -1, 1, 2)


def dot(lhs, rhs, lhs_axis=1, rhs_axis=0):
    return lax.dot_general(
        lhs, rhs, (((lhs_axis,), (rhs_axis,)), ((), ())), preferred_element_type=F32
    )


def step(index, by):
    return lax.rem(index + by + 4, 4)


class Here:
    def __init__(self):
        shard = lax.axis_index("shards")
        place = lax.axis_index("context")
        self.x, self.zl = lax.div(shard, 2), lax.rem(shard, 2)
        self.y, self.zh = lax.div(place, 4), lax.rem(lax.div(place, 2), 2)
        self.core = lax.rem(place, 2)
        self.z = self.zh * 2 + self.zl

    def at(self, dx=0, dy=0, dz=0, other_core=False):
        x, y, z = (lax.rem(v + d + 4, 4) for v, d in ((self.x, dx), (self.y, dy), (self.z, dz)))
        core = 1 - self.core if other_core else self.core
        return (x * 2 + lax.rem(z, 2), y * 4 + lax.div(z, 2) * 2 + core)


class Mail:
    def __init__(self, send, receive, like, device):
        self.send, self.receive, self.like, self.device = send, receive, like, device
        self.forms, self.gone = [], set()

    def reserve(self, shape, dtype):
        self.forms.append((shape, dtype))
        return len(self.forms) - 1

    def post(self, source, target, device, k=None):
        if k is None:
            k = self.reserve(source.shape, source.dtype)
        pltpu.make_async_remote_copy(
            src_ref=source,
            dst_ref=target,
            send_sem=self.send.at[k],
            recv_sem=self.receive.at[k],
            device_id=device,
            device_id_type=MESH,
        ).start()
        return k

    def sent(self, k):
        ref = self.like(*self.forms[k])
        return pltpu.make_async_remote_copy(
            src_ref=ref,
            dst_ref=ref,
            send_sem=self.send.at[k],
            recv_sem=self.receive.at[k],
            device_id=self.device,
            device_id_type=MESH,
        )

    def take(self, *posts):
        for k in posts:
            self.sent(k).wait_recv()

    def finish(self, count=None):
        for k in range(len(self.forms) if count is None else count):
            if k not in self.gone:
                self.sent(k).wait_send()
                self.gone.add(k)


def at_step(n, actions):
    for m, action in enumerate(actions):
        if action is not None:
            pl.when(n == m)(action)


def tell(semaphore, devices):
    for device in devices:
        pl.semaphore_signal(semaphore, inc=1, device_id=device, device_id_type=MESH)


class RingGather:
    def __init__(self, mail, place, me, right, left):
        self.mail, self.place, self.me, self.right, self.left = mail, place, me, right, left

    def post(self, half, to, source=None):
        ref = self.place(self.me if source is None else source, half)
        return self.mail.post(ref, ref, to)

    def start(self):
        self.from_left = [self.post(0, self.right), None]
        self.from_right = [None, self.post(1, self.left)]
        self.from_left[1] = self.post(1, self.right)
        self.from_right[0] = self.post(0, self.left)

    def start_half(self, half):
        if half == 0:
            self.from_left, self.from_right = [self.post(0, self.right), None], [None, None]
        else:
            self.from_right[1] = self.post(1, self.left)
            self.from_left[1] = self.post(1, self.right)
            self.from_right[0] = self.post(0, self.left)

    def relay(self):
        self.relay_half(0)
        self.relay_half(1)

    def relay_half(self, half):
        if half == 0:
            self.mail.take(self.from_left[0])
            self.opposite = [self.post(0, self.right, step(self.me, -1))]
        else:
            self.mail.take(self.from_right[1])
            self.opposite.append(self.post(1, self.left, step(self.me, 1)))

    def near(self):
        self.mail.take(self.from_left[1], self.from_right[0])

    def far(self):
        self.mail.take(*self.opposite)


class RingReduce:
    def __init__(self, mail, part, slots, me, right, left):
        self.mail, self.part, self.slots = mail, part, slots
        self.me, self.right, self.left = me, right, left

    def start_far(self, ready=lambda half: None):
        far = step(self.me, 2)
        self.relays = []
        for half, to in ((0, self.right), (1, self.left)):
            ready(half)
            self.relays.append(self.mail.post(self.part(far, half), self.slots(half), to))

    def start_right(self):
        self.arrivals = [self.mail.post(self.part(step(self.me, 1), 1), self.slots(2), self.right)]

    def start_left(self):
        self.arrivals.append(self.mail.post(self.part(step(self.me, -1), 0), self.slots(3), self.left))

    def start_near(self):
        self.start_right()
        self.start_left()

    def relay_half(self, half):
        near, to = ((step(self.me, 1), self.right), (step(self.me, -1), self.left))[half]
        self.mail.take(self.relays[half])
        ref = self.part(near, half)
        ref[...] = (ref[...].astype(F32) + self.slots(half)[...].astype(F32)).astype(BF16)
        self.arrivals.append(self.mail.post(ref, self.slots(4 + half), to))

    def relay(self):
        self.relay_half(0)
        self.relay_half(1)

    def total(self, half, own=None):
        first, second = ((4, 2), (3, 1)) if half == 0 else ((2, 0), (5, 3))
        self.mail.take(self.arrivals[first[1]], self.arrivals[second[1]])
        own = self.part(self.me, half)[...].astype(F32) if own is None else own
        return own + self.slots(first[0])[...].astype(F32) + self.slots(second[0])[...].astype(F32)


class RowsGather:
    def __init__(self, here, mail, buf):
        self.here, self.mail, self.buf = here, mail, buf
        self.partner = here.at(other_core=True)
        self.relayed = self.nearby = False
        self.ring = RingGather(mail, self.place, here.y, here.at(dy=1), here.at(dy=-1))

    def place(self, i, half):
        return self.buf.at[i, self.here.core, pl.ds(half * 64, 64)]

    def share(self, d, half):
        ref = self.place(step(self.here.y, d), half)
        return self.mail.post(ref, ref, self.partner)

    def start_half(self, half):
        self.ring.start_half(half)
        if half == 0:
            self.shared = []
        self.shared.append(self.share(0, half))

    def start(self):
        self.start_half(0)
        self.start_half(1)

    def relay(self):
        self.ring.relay_half(0)
        self.shared.append(self.share(-1, 0))
        self.ring.relay_half(1)
        self.shared.append(self.share(1, 1))
        self.relayed = True

    def near(self):
        if not self.relayed:
            self.relay()
        self.nearby = True
        self.mail.take(self.ring.from_left[1])
        self.shared.append(self.share(-1, 1))
        self.mail.take(self.ring.from_right[0])
        self.shared.append(self.share(1, 0))

    def far(self):
        for half in range(2):
            self.mail.take(self.ring.opposite[half])
            self.shared.append(self.share(2, half))

    def ready(self, d):
        first = {0: (0, 1), -1: (2, 4), 1: (3, 5), 2: (6, 7)}[d]
        self.mail.take(*(self.shared[k] for k in first))


class RowsReduce:
    def __init__(self, here, mail, part, from_partner, summed, slots):
        self.here, self.mail = here, mail
        self.part, self.from_partner, self.summed = part, from_partner, summed
        self.partner = here.at(other_core=True)
        self.halves = {2: (0, 1), 1: (1, 0), -1: (0, 1), 0: (0, 1)}
        self.ring = RingReduce(
            mail,
            lambda i, half: summed.at[i, pl.ds(half * 64, 64)],
            lambda k: slots.at[k],
            here.y,
            here.at(dy=1),
            here.at(dy=-1),
        )
        self.posts = {d: [mail.reserve((64, 1024), BF16) for _ in range(2)] for d in ORDER}

    def chunk(self, d):
        i = step(self.here.y, d)
        for half in self.halves[d]:
            rows = pl.ds(half * 64, 64)
            self.mail.post(
                self.part.at[i, 1 - self.here.core, rows],
                self.from_partner.at[i, rows],
                self.partner,
                self.posts[d][half],
            )

    def pair(self, d, half):
        i, rows = step(self.here.y, d), pl.ds(half * 64, 64)
        self.mail.take(self.posts[d][half])
        return self.part[i, self.here.core, rows].astype(F32) + self.from_partner[i, rows].astype(F32)

    def add(self, d, half):
        self.summed[step(self.here.y, d), pl.ds(half * 64, 64)] = self.pair(d, half).astype(BF16)

    def send_far(self):
        self.ring.start_far(lambda half: self.add(2, half))

    def send_right(self):
        self.add(1, 1)
        self.ring.start_right()
        self.add(1, 0)

    def send_left(self):
        self.add(-1, 0)
        self.ring.start_left()
        self.ring.relay_half(0)
        self.add(-1, 1)
        self.ring.relay_half(1)

    def totals(self):
        for half in range(2):
            yield half, self.ring.total(half, self.pair(0, half))


def row_halves(begin, first, second):
    starts = (begin, begin + first, begin + 2 * first, begin + 2 * first + second)
    return lambda part, half: pl.ds(starts[2 * part + half], (first, second)[part])


def split(j):
    return lax.div(j, 2), lax.rem(j, 2)


class WeightGather:
    def __init__(self, here, mail, buf, begin, first, second):
        along_x = (here.x, here.at(dx=1), here.at(dx=-1))
        along_z = (here.z, here.at(dz=1), here.at(dz=-1))
        rows = row_halves(begin, first, second)
        self.rings = (
            RingGather(mail, lambda i, h: buf.at[i, here.zh, here.zl, rows(0, h)], *along_x),
            RingGather(mail, lambda j, h: buf.at[(here.x, *split(j), rows(1, h))], *along_z),
            RingGather(mail, lambda j, h: buf.at[(slice(None), *split(j), rows(0, h))], *along_z),
            RingGather(mail, lambda i, h: buf.at[i, :, :, rows(1, h)], *along_x),
        )

    def start(self):
        self.rings[0].start()
        self.rings[1].start()

    def relay(self):
        self.rings[0].relay()
        self.rings[1].relay()

    def turn(self, parts=(0, 1)):
        for part in parts:
            self.rings[part].near()
            self.rings[part].far()
            self.rings[part + 2].start()

    def late(self, parts=(0, 1)):
        for part in parts:
            self.rings[part + 2].relay()

    def end(self):
        for ring in self.rings[2:]:
            ring.near()
            ring.far()


class WeightReduce:
    def __init__(self, here, mail, part, begin, first, second, slots):
        along_x = (here.x, here.at(dx=1), here.at(dx=-1))
        along_z = (here.z, here.at(dz=1), here.at(dz=-1))
        slots_z, slots_x, slots_third, slots_fourth = slots
        rows = row_halves(begin, first, second)
        self.rows, self.x, self.z = rows, here.x, (here.zh, here.zl)
        self.first = RingReduce(
            mail, lambda j, k: part.at[(slice(None), *split(j), rows(0, k))], lambda k: slots_z.at[k], *along_z
        )
        self.second = RingReduce(
            mail, lambda i, k: part.at[i, :, :, rows(1, k)], lambda k: slots_x.at[k], *along_x
        )
        self.third = RingReduce(
            mail,
            lambda i, k: part.at[i, here.zh, here.zl, rows(0, k)],
            lambda k: slots_third.at[k],
            *along_x,
        )
        self.fourth = RingReduce(
            mail,
            lambda j, k: part.at[(here.x, *split(j), rows(1, k))],
            lambda k: slots_fourth.at[k],
            *along_z,
        )
        self.part = part

    def start(self):
        for ring in (self.first, self.second):
            ring.start_far()
        for ring in (self.first, self.second):
            ring.start_near()

    def relay(self):
        for ring in (self.first, self.second):
            ring.relay()

    def turn(self):
        for half in range(2):
            self.part[(slice(None), *self.z, self.rows(0, half))] = self.first.total(half).astype(BF16)
            self.part[self.x, :, :, self.rows(1, half)] = self.second.total(half).astype(BF16)
        for ring in (self.third, self.fourth):
            ring.start_far()
        for ring in (self.third, self.fourth):
            ring.start_near()

    def late(self):
        for ring in (self.third, self.fourth):
            ring.relay()

    def end(self, out):
        for half in range(2):
            out[self.rows(0, half)] = self.third.total(half)
            out[self.rows(1, half)] = self.fourth.total(half)


def reduce_slots(name, first, second):
    return {
        name + "_z": ((6, 4, first, 128), BF16),
        name + "_x": ((6, 2, 2, second, 128), BF16),
        name + "_third": ((6, first, 128), BF16),
        name + "_fourth": ((6, second, 128), BF16),
    }


def ways(k):
    if k < 2:
        return ((0, 128, 1), (128, 128, -1))
    return ((0, 64, 1), (128, 64, -1), (64, 64, 1), (192, 64, -1))


class Swap:
    def __init__(self, here, mail, relays):
        self.here, self.mail, self.relays = here, mail, relays
        self.hops, self.arrivals = (
            [[mail.reserve((rows, 256), BF16) for _, rows, _ in ways(k)] for k in range(4)] for _ in range(2)
        )

    def post(self, k, source):
        for side, (begin, count, d) in enumerate(ways(k)):
            rows = pl.ds(begin, count)
            self.mail.post(
                source.at[rows], self.relays.at[k, rows], self.here.at(dz=d), self.hops[k][side]
            )

    def relay(self, k, target):
        for side, (begin, count, d) in enumerate(ways(k)):
            rows = pl.ds(begin, count)
            self.mail.take(self.hops[k][side])
            place = target(lax.div(step(self.here.z, -d), 2))
            self.mail.post(
                self.relays.at[k, rows], place.at[rows], self.here.at(dz=d), self.arrivals[k][side]
            )

    def arrived(self, k):
        self.mail.take(*self.arrivals[k])


def column_sum(value):
    return jnp.sum(value.reshape(-1, 8, value.shape[1]), axis=0)


def column_max(value):
    return jnp.max(value.reshape(-1, 8, value.shape[1]), axis=0)


def turn(section, cosine, sine):
    front, back = section[0:8], section[8:16]
    return jnp.concatenate(
        [front * cosine - back * sine, back * cosine + front * sine, section[ROT:]], axis=0
    )


def two_blocks(first, second):
    zero = jnp.zeros_like(first)
    return jnp.concatenate(
        [jnp.concatenate([first, zero], axis=1), jnp.concatenate([zero, second], axis=1)], axis=0
    )


def vector_row(kind, layer):
    return 8 * (kind if kind < 2 and layer == 0 else (2 + kind if layer else 5))


class Program:
    def __init__(self, refs):
        self.__dict__.update(refs)
        self.here = Here()
        self.near_x = [self.here.at(dx=d) for d in (1, -1)]
        self.near_y = [self.here.at(dy=d) for d in (1, -1)]
        self.near_z = [self.here.at(dz=d) for d in (1, -1)]
        self.partner = self.here.at(other_core=True)
        self.far = [self.here.at(dx=2), self.here.at(dy=2), self.here.at(dz=2)]
        self.reduced = 0
        self.mail = Mail(self.send, self.receive, self.like, self.partner)


    def like(self, shape, dtype):
        if dtype == F32:
            return self.vectors.at[0, 0 : shape[0]] if shape[0] <= 64 else self.vector_whole.at[0, 0 : shape[0]]
        if shape[-1] == 1024:
            return self.part.at[0, 0, 0 : shape[0]]
        if shape[-1] == 256:
            return self.relays.at[0, 0, 0 : shape[0]]
        rows = slice(0, shape[-2])
        return {
            2: lambda: self.weights.at[0, 0, 0, 0, rows],
            3: lambda: self.weights.at[0, :, 0, 0, rows],
            4: lambda: self.weights.at[0, 0, :, :, rows],
        }[len(shape)]()

    def ordered(self, k):
        return lax.rem(self.here.y + jnp.where(k == 0, 2, jnp.where(k == 1, 1, jnp.where(k == 2, 3, 0))), 4)

    def arriving(self, n):
        return lax.rem(self.here.y + jnp.where(n == 0, 0, jnp.where(n == 1, 3, jnp.where(n == 2, 1, 2))), 4)

    def weight(self, layer, rows):
        return jnp.concatenate(
            [
                jnp.concatenate(
                    [self.weights[layer, x, zh, half, rows] for half in range(2) for x in range(4)], axis=1
                )
                for zh in range(2)
            ],
            axis=0,
        )

    def chunk(self, buf, i):
        return buf[i].reshape(256, 1024)

    def chunk_pair(self, buf, pair):
        return buf[pl.ds(pair * 2, 2)].reshape(512, 1024)

    def arrange(self, ref):
        return jnp.concatenate(
            [ref[:, (x * 2 + zl) * 128 : (x * 2 + zl) * 128 + 128] for zl in range(2) for x in range(4)],
            axis=1,
        )

    def restore(self, ref, value):
        for zl in range(2):
            for x in range(4):
                ref[:, (x * 2 + zl) * 128 : (x * 2 + zl) * 128 + 128] = value[
                    :, (zl * 4 + x) * 128 : (zl * 4 + x) * 128 + 128
                ]

    def keep_sum(self, kind, layer, value):
        for zl in range(2):
            for x in range(4):
                row = vector_row(kind, layer) + x * 2 + zl
                self.vectors[0, row : row + 1, :] = value[:, (zl * 4 + x) * 128 : (zl * 4 + x) * 128 + 128]


    def norm(self, layer, half):
        rows = slice(half * 64, half * 64 + 64)
        rows_in = self.stream[rows]
        centered = rows_in - jnp.mean(rows_in, axis=-1, keepdims=True)
        variance = jnp.mean(centered * centered, axis=-1, keepdims=True)
        inverse = lax.rsqrt(variance + EPSILON)
        normal = centered * inverse
        self.normal[layer, rows] = normal
        self.inverse[layer, rows] = jnp.broadcast_to(inverse, (64, 128))
        normed = normal * self.vector(self.gain, layer) + self.vector(self.shift, layer)
        self.rows[layer, self.here.y, self.here.core, rows] = normed.astype(BF16)

    def vector(self, ref, layer):
        return self.arrange(ref.at[layer : layer + 1])

    def prepare(self, layer):
        here = self.here
        own = self.weights.at[layer, here.x, here.zh, here.zl]
        own[0:192] = self.qkv_weight[layer]
        own[192:448] = self.fc1_weight[layer].T
        own[448:512] = self.out_weight[layer]
        own[512:768] = self.fc2_weight[layer]

    def prepare_bias(self, layer):
        here = self.here
        for zh in range(2):
            head = here.y * 4 + zh * 2 + here.core
            first = self.qkv_bias[layer, pl.ds(head, 1), :]
            second = self.fc1_bias[layer : layer + 1, pl.ds(pl.multiple_of(head * 256, 256), 256)]
            self.bias[zh, 0:192] = jnp.broadcast_to(first, (8, 192)).T
            self.bias[zh, 192:448] = jnp.broadcast_to(second, (8, 256)).T

    def project(self, layer, i):
        cosine, sine = self.angles[self.here.zh, 0, i], self.angles[self.here.zh, 1, i]
        keys, values, queries = [], [], []
        whole = dot(self.weight(layer, slice(0, 192)), self.chunk(self.rows.at[layer], i), 1, 1)
        for head in range(2):
            out = whole[head * 192 : head * 192 + 192] + self.bias[head, 0:192, 0:1]
            queries.append((turn(out[0:64], cosine, sine) * HD**-0.5).astype(BF16))
            keys.append(turn(out[64:128], cosine, sine).astype(BF16))
            values.append(out[128:192].astype(BF16))
        self.queries[layer, i] = two_blocks(*queries)
        both = jnp.concatenate(keys + values, axis=0)
        here = i * 2 + self.here.zh
        self.across[layer, here] = both
        self.along[layer, here] = both.T

    def units(self, layer, pair):
        whole = dot(self.weight(layer, slice(192, 448)), self.chunk_pair(self.rows.at[layer], pair), 1, 1)
        for place in range(2):
            i = pair * 2 + place
            for zh in range(2):
                hidden = whole[zh * 256 : zh * 256 + 256, place * 256 : place * 256 + 256]
                hidden = hidden + self.bias[zh, 192:448, 0:1]
                cumulative = 0.5 + 0.5 * lax.erf(hidden * 0.5**0.5)
                slope = cumulative + hidden * (jnp.exp(-0.5 * hidden * hidden) * (2.0 * np.pi) ** -0.5)
                self.slope[layer, i, zh] = slope.astype(BF16)
                self.into_out[layer, i, zh, 64:320] = (hidden * cumulative).astype(BF16)

    def prepare_mask(self):
        key = lax.broadcasted_iota(jnp.int32, (512, 256), 0)
        query = lax.broadcasted_iota(jnp.int32, (512, 256), 1)
        self.mask[0] = jnp.zeros((512, 256), F32)
        self.mask[1] = jnp.where(key <= query + self.here.zh * 256, 0.0, MASKED)

    def score(self, layer, i, pair):
        keys = self.along[layer, pl.ds(pair * 2, 2), :, 0:128].reshape(512, 128)
        mask = self.mask[jnp.where(i == pair, 1, 0)]
        return dot(keys, self.queries[layer, i]) + jnp.concatenate([mask, mask], axis=1)

    def clear_attention(self):
        self.peaks[...] = jnp.full((4, 8, 512), MASKED, F32)
        self.totals[...] = jnp.zeros((4, 8, 512), F32)
        self.mixed[...] = jnp.zeros((4, 128, 256), F32)

    def attend(self, layer, i, pair):
        scores = self.score(layer, i, pair)
        before = self.peaks[i, 0:1]
        peak = jnp.maximum(before, jnp.max(column_max(scores), axis=0, keepdims=True))
        shrink = jnp.exp(before - peak)
        terms = jnp.exp(scores - peak)
        self.peaks[i] = jnp.broadcast_to(peak, (8, 512))
        self.totals[i] = self.totals[i] * shrink + column_sum(terms)
        low = terms.astype(BF16)
        for head in range(2):
            rows = slice(128 + head * 64, 192 + head * 64)
            at = slice(head * 256, head * 256 + 256)
            values = jnp.concatenate(
                [self.across[layer, pair * 2, rows], self.across[layer, pair * 2 + 1, rows]], axis=1
            )
            mine = slice(head * 64, head * 64 + 64)
            self.mixed[i, mine] = self.mixed[i, mine] * shrink[:, at] + dot(values, low[:, at])

    def attended(self, layer, i):
        total = jnp.sum(self.totals[i], axis=0, keepdims=True)
        for head in range(2):
            self.into_out[layer, i, head, 0:64] = (
                self.mixed[i, head * 64 : head * 64 + 64] / total[:, head * 256 : head * 256 + 256]
            ).astype(BF16)
        self.logs[layer, i] = jnp.broadcast_to(self.peaks[i, 0:1] + jnp.log(total), (8, 512))

    def each_unit(self, k, work):
        mine = self.ordered(k)

        def one(later, _):
            other = self.ordered(later)
            work(jnp.maximum(mine, other), jnp.minimum(mine, other), later)
            return 0

        lax.fori_loop(k, 4, one, 0)

    def spread_rows(self, i, units, layer, rows):
        value = dot(units.T, self.weight(layer, rows)).astype(BF16)
        self.part[i] = value.reshape(2, 128, 1024)

    def rows_reduce(self):
        self.mail.finish(self.reduced)
        return RowsReduce(self.here, self.mail, self.part, self.from_partner, self.summed, self.slots)

    def project_all(self, layer, gather, between):
        here = self.here
        self.mail.finish(self.reduced)
        self.swap = swap = Swap(here, self.mail, self.relays.at[layer])

        def near():
            if not gather.nearby:
                gather.near()

        def post(n):
            def run():
                swap.post(n, self.across.at[layer, step(here.y, ARRIVAL[n]) * 2 + here.zh])
                between[n]()

            return run

        def one(n, _):
            at_step(n, [None, near, None, gather.far])
            at_step(n, [lambda d=d: gather.ready(d) for d in ARRIVAL])
            self.project(layer, self.arriving(n))
            at_step(n, [post(m) for m in range(4)])
            return 0

        lax.fori_loop(0, 4, one, 0)

    def swap_relay(self, layer, n):
        i = step(self.here.y, ARRIVAL[n])
        self.swap.relay(n, lambda zh: self.across.at[layer, i * 2 + zh])

    def swapped(self, layer):
        def one(n, _):
            at_step(n, [lambda m=m: self.swap.arrived(m) for m in range(4)])
            other = self.arriving(n) * 2 + 1 - self.here.zh
            self.along[layer, other] = self.across[layer, other].T
            return 0

        lax.fori_loop(0, 4, one, 0)

    def mix(self, layer, hooks):
        reduce = self.rows_reduce()
        due = {(1, 3): reduce.send_far, (2, 3): reduce.send_right, (3, 3): reduce.send_left}

        def one(k, _):
            def unit(i, pair, later):
                self.attend(layer, i, pair)
                for table in (due, hooks):
                    for (first, second), action in table.items():
                        pl.when(jnp.logical_and(k == first, later == second))(action)

            self.each_unit(k, unit)
            i = self.ordered(k)
            self.attended(layer, i)
            self.spread_rows(i, self.into_out[layer, i].reshape(640, 256), layer, OUT_ROWS)
            at_step(k, [lambda d=d: reduce.chunk(d) for d in ORDER])
            return 0

        lax.fori_loop(0, 4, one, 0)
        return reduce


    def grads_of_pair(self, layer, pair):
        whole = dot(self.weight(layer, OUT_ROWS), self.chunk_pair(self.grad_rows.at[layer], pair), 1, 1)
        unit_grads = []
        for place in range(2):
            at = slice(place * 256, place * 256 + 256)
            self.mixed_grads[pair * 2 + place] = two_blocks(
                *(whole[zh * 320 : zh * 320 + 64, at].astype(BF16) for zh in range(2))
            )
            unit_grads.append([whole[zh * 320 + 64 : zh * 320 + 320, at] for zh in range(2)])
        return unit_grads

    def slope_of_chunk(self, layer, i, unit_grads):
        deltas = []
        for zh in range(2):
            both = self.mixed_grads[i, zh * 64 : zh * 64 + 64, zh * 256 : zh * 256 + 256].astype(F32)
            both = both * self.into_out[layer, i, zh, 0:64].astype(F32)
            deltas.append(jnp.sum(both, axis=0, keepdims=True))
            self.into_in[i, zh, 192:448] = (
                unit_grads[zh] * self.slope[layer, i, zh].astype(F32)
            ).astype(BF16)
        self.delta[i] = jnp.broadcast_to(jnp.concatenate(deltas, axis=1), (8, 512))
        self.mixed_grads_along[i] = self.mixed_grads[i].T
        self.queries_along[i] = self.queries[layer, i].T

    def grads_ahead(self, layer, pair):
        for place, unit_grads in enumerate(self.grads_of_pair(layer, pair)):
            for zh in range(2):
                self.into_in[pair * 2 + place, zh, 192:448] = unit_grads[zh].astype(BF16)

    def slope_after(self, layer, i):
        self.slope_of_chunk(layer, i, [self.into_in[i, zh, 192:448].astype(F32) for zh in range(2)])

    def grads_now(self, layer, pair):
        for place, unit_grads in enumerate(self.grads_of_pair(layer, pair)):
            self.slope_of_chunk(layer, pair * 2 + place, unit_grads)

    def weight_grads(self, layer, units, buf, rows):
        lhs = jnp.concatenate([units(zh) for zh in range(2)], axis=0)
        count = rows.stop - rows.start
        value = dot(lhs, buf[layer].reshape(1024, 1024)).astype(BF16)
        for zh in range(2):
            for half in range(2):
                for x in range(4):
                    self.weight_part[layer, x, zh, half, rows] = value[
                        zh * count : zh * count + count, half * 512 + x * 128 : half * 512 + x * 128 + 128
                    ]

    def clear_grads(self):
        def one(i, _):
            self.pair_grads[i] = jnp.zeros((512, 256), F32)
            self.grad_queries[i] = jnp.zeros((128, 256), F32)
            return 0

        lax.fori_loop(0, 4, one, 0)

    def attend_back(self, layer, i, pair):
        values = self.along[layer, pl.ds(pair * 2, 2), :, 128:256].reshape(512, 128)
        scores = self.score(layer, i, pair)
        probs = jnp.exp(scores - self.logs[layer, i, 0:1])
        grad_probs = dot(values, self.mixed_grads[i])
        grad_scores = (probs * (grad_probs - self.delta[i, 0:1])).astype(BF16)
        self.pair_grads[pair, :, 128:256] += dot(probs.astype(BF16), self.mixed_grads_along[i])
        self.pair_grads[pair, :, 0:128] += dot(grad_scores, self.queries_along[i])
        across = jnp.concatenate(
            [self.across[layer, pair * 2, 0:128], self.across[layer, pair * 2 + 1, 0:128]], axis=1
        )
        for head in range(2):
            rows = slice(head * 64, head * 64 + 64)
            self.grad_queries[i, rows] += dot(across[rows], grad_scores[:, head * 256 : head * 256 + 256])

    def half_of_pair(self, i, zh):
        return self.pair_grads[i, pl.ds(pl.multiple_of(zh * 256, 256), 256)]

    def send_pair(self, k):
        i = step(self.here.y, ORDER[k])
        self.sent_grads[i] = self.half_of_pair(i, 1 - self.here.zh).astype(BF16)
        self.swap.post(k, self.sent_grads.at[i])

    def relay_pair(self, layer, k):
        i = step(self.here.y, ORDER[k])
        self.swap.relay(k, lambda zh: self.other_grads.at[layer, i])

    def grad_project(self, layer, i):
        cosine, sine = self.angles[self.here.zh, 0, i], self.angles[self.here.zh, 1, i]
        summed = (self.half_of_pair(i, self.here.zh) + self.other_grads[layer, i].astype(F32)).T
        for head in range(2):
            rows = slice(head * 64, head * 64 + 64)
            self.into_in[i, head, 0:64] = turn(
                self.grad_queries[i, rows] * HD**-0.5, cosine, -sine
            ).astype(BF16)
            self.into_in[i, head, 64:128] = turn(summed[rows], cosine, -sine).astype(BF16)
            self.into_in[i, head, 128:192] = summed[128 + head * 64 : 192 + head * 64].astype(BF16)

    def keep_unit_sums(self, layer):
        ones = jnp.ones((8, 256), BF16)
        for zh in range(2):
            value = sum(dot(ones, self.into_in[i, zh], 1, 1) for i in range(4))[0:1]
            value = jnp.concatenate([value, jnp.zeros((1, 64), F32)], axis=1)
            for k in range(4):
                row = 48 + (layer * 2 + zh) * 4 + k
                self.vectors[0, row : row + 1, :] = value[:, k * 128 : k * 128 + 128]

    def weight_grads_out(self, layer):
        self.weight_grads(
            layer,
            lambda zh: jnp.concatenate([self.into_out[layer, i, zh] for i in range(4)], axis=1),
            self.grad_rows,
            OUT_ROWS,
        )

    def weight_grads_in(self, layer, rows):
        self.weight_grads(
            layer,
            lambda zh: jnp.concatenate([self.into_in[i, zh, rows] for i in range(4)], axis=1),
            self.rows,
            rows,
        )

    def backward(self, layer, hooks, fill):
        self.swap = Swap(self.here, self.mail, self.relays.at[LAYERS - 1 - layer])
        reduce = self.rows_reduce()
        if layer == LAYERS - 1:
            pl.semaphore_wait(self.credit, 3)

        def after(k):
            def run():
                self.send_pair(k)
                if k < 3:
                    hooks[k]()

            return run

        def attention(k, _):
            def unit(i, pair, later):
                self.attend_back(layer, i, pair)
                for m in range(1, 4):
                    due = min(m + 1, 3)
                    pl.when(jnp.logical_and(k == m, later == due))(lambda m=m: self.relay_pair(layer, m - 1))

            self.each_unit(k, unit)
            at_step(k, [after(m) for m in range(4)])
            return 0

        def first():
            self.swap.arrived(0)

        def second():
            self.swap.arrived(1)

        def third():
            self.relay_pair(layer, 3)
            self.swap.arrived(2)

        def fourth():
            fill[0]()
            self.swap.arrived(3)

        def second_out():
            reduce.chunk(ORDER[1])
            reduce.send_far()

        def third_out():
            reduce.chunk(ORDER[2])
            reduce.send_right()

        def fourth_out():
            reduce.chunk(ORDER[3])
            reduce.send_left()

        def rows_of(n, _):
            i = self.ordered(n)
            at_step(n, [first, second, third, fourth])
            self.grad_project(layer, i)
            self.spread_rows(i, self.into_in[i].reshape(896, 256), layer, IN_ROWS)
            at_step(n, [lambda: reduce.chunk(ORDER[0]), second_out, third_out, fourth_out])
            return 0

        def both(k, _):
            @pl.when(k == 3)
            def _():
                rows_of(0, 0)

            return attention(k, 0)

        lax.fori_loop(0, 4, both, 0)
        lax.fori_loop(1, 4, rows_of, 0)
        fill[1]()
        return reduce

    def norm_back(self, layer, half, grad_normed, sums):
        rows = slice(half * 64, half * 64 + 64)
        normal, inverse = self.normal[layer, rows], self.inverse[layer, rows, 0:1]
        sums[0] = sums[0] + jnp.sum(grad_normed * normal, axis=0, keepdims=True)
        sums[1] = sums[1] + jnp.sum(grad_normed, axis=0, keepdims=True)
        scaled = grad_normed * self.vector(self.gain, layer)
        first_mean = jnp.mean(scaled, axis=-1, keepdims=True)
        cross_mean = jnp.mean(scaled * normal, axis=-1, keepdims=True)
        return self.stream[rows] + inverse * (scaled - first_mean - normal * cross_mean)

    def round_rows(self, layer, half, grad, sums):
        rows = slice(half * 64, half * 64 + 64)
        low = grad.astype(BF16)
        self.grad_rows[layer, self.here.y, self.here.core, rows] = low
        sums[2] = sums[2] + jnp.sum(low.astype(F32), axis=0, keepdims=True)

    def weight_reduce(self, part, begin, first, second, name):
        slots = [getattr(self, name + "_" + kind) for kind in ("z", "x", "third", "fourth")]
        return WeightReduce(self.here, self.mail, part, begin, first, second, slots)

    def sum_vectors(self, begin, count, kept):
        here, mail = self.here, self.mail
        summed = count - kept
        rows = pl.ds(begin, count)

        def slot(k):
            return self.vector_slots.at[k, rows]

        for stage, axis in enumerate(("dx", "dz")):
            posts = [
                mail.post(self.vectors.at[stage, rows], slot(3 * stage + d - 1), here.at(**{axis: d}))
                for d in (1, 2, 3)
            ]
            yield
            mail.take(*posts)
            self.vectors[stage + 1, rows] = self.vectors[stage, rows] + sum(
                slot(3 * stage + d)[...] for d in range(3)
            )
        posts = [
            mail.post(self.vectors.at[2, rows], slot(6 + d - 1), here.at(dy=d)) for d in (1, 2, 3)
        ]
        yield
        mail.take(*posts)
        whole = self.vector_whole
        self.vector_whole[0, begin : begin + summed] = self.vectors[2, begin : begin + summed] + sum(
            self.vector_slots[6 + d, begin : begin + summed] for d in range(3)
        )
        total = summed
        if kept:
            total = summed + 4 * kept
            first, last = begin + summed, begin + count
            whole[0, pl.ds(first + here.y * kept, kept)] = self.vectors[2, first:last]
            for d in (1, 2, 3):
                whole[0, pl.ds(first + step(here.y, -d) * kept, kept)] = self.vector_slots[
                    6 + d - 1, first:last
                ]
        rows_out = pl.ds(begin, total)
        last = mail.post(whole.at[0, rows_out], whole.at[1, rows_out], self.partner)
        yield
        mail.take(last)
        yield

    def write_vectors(self, whole):
        for kind, out in enumerate((self.gain_out, self.shift_out, self.bias_out)):
            for layer in range(LAYERS):
                for s in range(8):
                    row = vector_row(kind, layer) + s
                    out[layer : layer + 1, s * 128 : s * 128 + 128] = (
                        whole[0, row : row + 1] + whole[1, row : row + 1]
                    )
        for source in range(2):
            core = self.here.core if source == 0 else 1 - self.here.core
            for y in range(4):
                for layer in range(LAYERS):
                    for zh in range(2):
                        head = y * 4 + zh * 2 + core
                        row = 48 + y * 16 + (layer * 2 + zh) * 4
                        wide = jnp.concatenate(
                            [whole[source, row + k : row + k + 1] for k in range(4)], axis=1
                        )
                        self.qkv_bias_out[layer, pl.ds(head, 1), :] = wide[:, 0:192]
                        self.fc1_bias_out[
                            layer : layer + 1, pl.ds(pl.multiple_of(head * 256, 256), 256)
                        ] = wide[:, 192:448]

    def write_weights(self, layer, rows):
        owned = self.owned.at[layer]
        if rows == IN_ROWS:
            self.qkv_out[layer] = owned[0:192]
            return
        self.fc1_out[layer] = owned[192:448].T
        self.out_out[layer] = owned[448:512]
        self.fc2_out[layer] = owned[512:768]


    def run(self):
        here, mail = self.here, self.mail
        barrier = pltpu.get_barrier_semaphore()
        everyone = self.near_x + self.near_y + self.near_z + [self.partner] + self.far
        tell(barrier, everyone)
        self.prepare(0)
        self.prepare_mask()
        self.stream[...] = self.arrange(self.hidden_in).astype(F32)
        for half in range(2):
            self.norm(0, half)
        zero = jnp.zeros((1, 1024), F32)
        sums = [zero, zero, zero]
        for half in range(2):
            self.round_rows(
                1, half, self.arrange(self.cotangent.at[half * 64 : half * 64 + 64]).astype(F32), sums
            )
        self.keep_sum(2, 1, sums[2])
        pl.semaphore_wait(barrier, len(everyone))

        def gather_weights(layer, begin, first, second):
            return WeightGather(here, mail, self.weights.at[layer], begin, first, second)

        def nothing():
            pass

        ahead = gather_weights(0, 0, 48, 48)
        rest = gather_weights(0, 192, 64, 224)
        later = gather_weights(1, 0, 192, 192)
        ahead.start()
        gather = RowsGather(here, mail, self.rows.at[0])
        gather.start()
        rest.start()
        self.prepare_bias(0)
        ahead.relay()
        ahead.turn()
        rest.relay()
        back = RowsGather(here, mail, self.grad_rows.at[1])
        ahead.late()
        gather.relay()
        rest.turn((1,))
        ahead.end()

        def after_near():
            self.swap_relay(0, 0)

        def after_far():
            self.swap_relay(0, 1)
            rest.late((1,))
            self.swap_relay(0, 2)

        self.project_all(0, gather, [nothing, nothing, after_near, after_far])
        back.start()
        self.clear_attention()
        self.prepare(1)
        self.swap_relay(0, 3)
        rest.turn((0,))
        self.swapped(0)

        def first_units():
            rest.late((0,))
            back.relay()

        def first_units_of(pair, _):
            self.units(0, pair)
            return 0

        def fourth_units():
            rest.end()
            later.start()
            lax.fori_loop(0, 2, first_units_of, 0)

        reduce = self.mix(
            0,
            {
                (0, 0): first_units,
                (0, 2): back.near,
                (0, 3): fourth_units,
                (1, 1): later.relay,
                (1, 2): back.far,
                (2, 2): later.turn,
                (3, 3): later.late,
            },
        )
        self.reduced = len(mail.forms)
        gather = RowsGather(here, mail, self.rows.at[1])
        for half, value in reduce.totals():
            rows = slice(half * 64, half * 64 + 64)
            bias = self.vector(self.out_bias, 0) + self.vector(self.fc2_bias, 0)
            self.stream[rows] = self.stream[rows] + value + bias
            self.norm(1, half)
            gather.start_half(half)
        later.end()
        for d in (0, -1, 1, 2):
            back.ready(d)
        self.prepare_bias(1)
        self.clear_attention()

        def ahead_of(n, _):
            self.grads_ahead(1, n)
            at_step(n, [gather.relay])
            return 0

        lax.fori_loop(0, 2, ahead_of, 0)
        self.project_all(
            1,
            gather,
            [
                nothing,
                lambda: self.swap_relay(1, 0),
                lambda: self.swap_relay(1, 1),
                lambda: self.swap_relay(1, 2),
            ],
        )

        def units_of(pair, _):
            self.units(1, pair)
            at_step(pair, [lambda: self.swap_relay(1, 3)])
            return 0

        lax.fori_loop(0, 2, units_of, 0)
        self.swapped(1)
        reduce = self.mix(1, {})
        self.clear_grads()

        def slope_of(i, _):
            self.slope_after(1, i)
            return 0

        lax.fori_loop(0, 4, slope_of, 0)
        for half, value in reduce.totals():
            rows = slice(half * 64, half * 64 + 64)
            bias = self.vector(self.out_bias, 1) + self.vector(self.fc2_bias, 1)
            self.restore(self.hidden_out.at[rows], (self.stream[rows] + value + bias).astype(BF16))
        self.reduced = len(mail.forms)
        tell(self.credit, self.near_y + [self.partner])

        self.stream[...] = self.arrange(self.cotangent).astype(F32)
        units = slice(192, 448)
        reduce = self.backward(
            1,
            [nothing] * 3,
            [lambda: self.weight_grads_out(1), lambda: self.weight_grads_in(1, units)],
        )
        self.reduced = len(mail.forms)
        sums = [zero, zero, zero]
        gather = RowsGather(here, mail, self.grad_rows.at[0])
        for half, value in reduce.totals():
            rows = slice(half * 64, half * 64 + 64)
            grad = self.norm_back(1, half, value, sums)
            self.round_rows(0, half, grad, sums)
            gather.start_half(half)
            self.stream[rows] = grad
        self.weight_grads_in(1, slice(0, 192))
        whole = self.weight_reduce(self.weight_part.at[1], 0, 192, 192, "whole")
        whole.start()
        self.keep_unit_sums(1)
        gather.relay()
        self.keep_sum(0, 1, sums[0])
        self.keep_sum(1, 1, sums[1])
        self.keep_sum(2, 0, sums[2])
        self.clear_grads()
        gather.near()

        def first_pair():
            for d in (0, -1, 1):
                gather.ready(d)

        def other_pair():
            gather.far()
            gather.ready(2)

        def grads_of(n, _):
            at_step(n, [first_pair, other_pair])
            self.grads_now(0, lax.rem(lax.div(here.y, 2) + n, 2))
            return 0

        whole.relay()
        lax.fori_loop(0, 2, grads_of, 0)
        self.weight_grads_out(0)
        self.weight_grads_in(0, units)
        whole.turn()
        early = self.weight_reduce(self.weight_part.at[0], 192, 64, 224, "early")
        early.start()
        late = self.weight_reduce(self.weight_part.at[0], 0, 48, 48, "late")

        def first_hook():
            whole.late()

        def second_hook():
            early.relay()

        def third_hook():
            whole.end(self.owned.at[1])
            self.write_weights(1, IN_ROWS)
            self.write_weights(1, OUT_ROWS)

        def first_fill():
            pass

        def second_fill():
            early.turn()
            self.weight_grads_in(0, slice(0, 192))
            late.start()
            self.keep_unit_sums(0)

        reduce = self.backward(0, [first_hook, second_hook, third_hook], [first_fill, second_fill])
        vectors = self.sum_vectors(16, 48, 16)
        next(vectors)
        early.late()
        sums = [zero, zero, zero]
        for half, value in reduce.totals():
            rows = slice(half * 64, half * 64 + 64)
            self.restore(self.grad_in.at[rows], self.norm_back(0, half, value, sums))
        self.keep_sum(0, 0, sums[0])
        self.keep_sum(1, 0, sums[1])
        last = self.sum_vectors(0, 16, 0)
        next(last)
        next(vectors)
        late.relay()
        early.end(self.owned.at[0])
        self.write_weights(0, OUT_ROWS)
        next(last)
        next(vectors)
        late.turn()
        next(last)
        next(vectors)
        late.late()
        next(last)
        next(vectors)
        late.end(self.owned.at[0])
        self.write_weights(0, IN_ROWS)
        next(last)
        self.write_vectors(self.vector_whole)
        mail.finish()


INPUTS = (
    "hidden_in", "cotangent", "qkv_weight", "fc1_weight", "out_weight", "fc2_weight",
    "gain", "shift", "qkv_bias", "fc1_bias", "out_bias", "fc2_bias", "angles",
)
OUTPUTS = {
    "hidden_out": ((128, 1024), BF16),
    "grad_in": ((128, 1024), F32),
    "gain_out": ((LAYERS, 1024), F32),
    "shift_out": ((LAYERS, 1024), F32),
    "qkv_out": ((LAYERS, 192, 128), F32),
    "qkv_bias_out": ((LAYERS, 16, 192), F32),
    "out_out": ((LAYERS, 64, 128), F32),
    "bias_out": ((LAYERS, 1024), F32),
    "fc1_out": ((LAYERS, 128, 256), F32),
    "fc1_bias_out": ((LAYERS, 4096), F32),
    "fc2_out": ((LAYERS, 256, 128), F32),
}
SCRATCH = {
    "weights": ((LAYERS, 4, 2, 2, 768, 128), BF16),
    "rows": ((LAYERS, 4, 2, 128, 1024), BF16),
    "grad_rows": ((LAYERS, 4, 2, 128, 1024), BF16),
    "stream": ((128, 1024), F32),
    "normal": ((LAYERS, 128, 1024), F32),
    "inverse": ((LAYERS, 128, 128), F32),
    "queries": ((LAYERS, 4, 128, 512), BF16),
    "across": ((LAYERS, 8, 256, 256), BF16),
    "along": ((LAYERS, 8, 256, 256), BF16),
    "slope": ((LAYERS, 4, 2, 256, 256), BF16),
    "into_out": ((LAYERS, 4, 2, 320, 256), BF16),
    "logs": ((LAYERS, 4, 8, 512), F32),
    "peaks": ((4, 8, 512), F32),
    "mask": ((2, 512, 256), F32),
    "totals": ((4, 8, 512), F32),
    "mixed": ((4, 128, 256), F32),
    "part": ((4, 2, 128, 1024), BF16),
    "from_partner": ((4, 128, 1024), BF16),
    "summed": ((4, 128, 1024), BF16),
    "slots": ((6, 64, 1024), BF16),
    "relays": ((2, 4, 256, 256), BF16),
    "delta": ((4, 8, 512), F32),
    "mixed_grads": ((4, 128, 512), BF16),
    "mixed_grads_along": ((4, 512, 128), BF16),
    "queries_along": ((4, 512, 128), BF16),
    "grad_queries": ((4, 128, 256), F32),
    "pair_grads": ((4, 512, 256), F32),
    "bias": ((2, 448, 8), F32),
    "owned": ((LAYERS, 768, 128), F32),
    "sent_grads": ((4, 256, 256), BF16),
    "other_grads": ((LAYERS, 4, 256, 256), BF16),
    "into_in": ((4, 2, 448, 256), BF16),
    "weight_part": ((LAYERS, 4, 2, 2, 768, 128), BF16),
    **reduce_slots("whole", 192, 192),
    **reduce_slots("early", 64, 224),
    **reduce_slots("late", 48, 48),
    "vectors": ((3, 64, 128), F32),
    "vector_slots": ((9, 64, 128), F32),
    "vector_whole": ((2, 112, 128), F32),
}
COPIES = 384


def kernel(*refs):
    names = (*INPUTS, *OUTPUTS, *SCRATCH, "send", "receive", "credit")
    Program(dict(zip(names, refs, strict=True))).run()


def hand_out(*refs):
    count = len(OUTPUTS)
    sources = [*refs[:count], refs[list(OUTPUTS).index("bias_out")]]
    for source, target in zip(sources, refs[count:], strict=True):
        target[...] = source[...]


def rotary_tables():
    frequency = 1.0 / 10000.0 ** (np.arange(0, ROT, 2).astype(np.float32) / np.float32(ROT))
    positions = (
        np.arange(4)[None, :, None] * 512 + np.arange(2)[:, None, None] * 256 + np.arange(256)
    ).astype(np.float32)
    angles = (positions[:, :, None, :] * frequency.astype(np.float32)[:, None]).astype(np.float64)
    return np.stack([np.cos(angles), np.sin(angles)], axis=1).astype(np.float32)


def on_device(
    hidden_in,
    ln_gain,
    ln_bias,
    qkv_weight,
    qkv_bias,
    out_weight,
    out_bias,
    fc1_weight,
    fc1_bias,
    fc2_weight,
    fc2_bias,
    cotangent,
):
    vmem = pl.BlockSpec(memory_space=pltpu.VMEM)
    shapes = [jax.ShapeDtypeStruct(*spec) for spec in OUTPUTS.values()]
    results = pl.pallas_call(
        kernel,
        out_shape=shapes,
        in_specs=[vmem] * len(INPUTS),
        out_specs=[vmem] * len(OUTPUTS),
        scratch_shapes=[pltpu.VMEM(*spec) for spec in SCRATCH.values()]
        + [pltpu.SemaphoreType.DMA((COPIES,))] * 2
        + [pltpu.SemaphoreType.REGULAR],
        compiler_params=pltpu.CompilerParams(
            collective_id=1, has_side_effects=True, vmem_limit_bytes=VMEM_LIMIT
        ),
    )(
        hidden_in[0],
        cotangent[0],
        qkv_weight.transpose(0, 2, 3, 1).reshape(LAYERS, 192, 128),
        fc1_weight,
        out_weight.reshape(LAYERS, 64, 128),
        fc2_weight,
        ln_gain,
        ln_bias,
        qkv_bias,
        fc1_bias,
        out_bias,
        fc2_bias,
        jnp.asarray(rotary_tables()),
    )
    bias = list(OUTPUTS).index("bias_out")
    sources = [*range(len(shapes)), bias]
    results = pl.pallas_call(
        hand_out,
        out_shape=[shapes[k] for k in sources],
        in_specs=[vmem] * len(shapes),
        out_specs=[vmem] * len(sources),
    )(*results)
    hidden_out, grad_in, gain, shift, qkv, qkv_sum, out, first, fc1, fc1_sum, fc2, second = results
    return (
        hidden_out[None],
        grad_in[None],
        gain,
        shift,
        qkv.reshape(LAYERS, 1, 192, 128).transpose(0, 3, 1, 2),
        qkv_sum,
        out.reshape(out_weight.shape),
        first,
        fc1,
        fc1_sum,
        fc2,
        second,
    )


def solution(mesh):
    placed = (
        P("shards", "context", None),
        P(),
        P(),
        P(None, "shards", "context", None),
        P(),
        P(None, "context", None, "shards"),
        P(),
        P(None, "shards", "context"),
        P(),
        P(None, "context", "shards"),
        P(),
        P("shards", "context", None),
    )
    return jax.shard_map(
        on_device,
        mesh=mesh,
        in_specs=placed,
        out_specs=(
            P("shards", "context", None),
            P("shards", "context", None),
            P(),
            P(),
            P(None, "shards", "context", None),
            P(),
            P(None, "context", None, "shards"),
            P(),
            P(None, "shards", "context"),
            P(),
            P(None, "context", "shards"),
            P(),
        ),
        check_vma=False,
    )
```
